128 devices in a mesh: snap: 16 (over x, z_hi, core), span: 8 (over y, z_lo).
Axes of the slice: x: 4, y: 4, z: 4 (z_hi: 2, z_lo: 2; z = z_hi * 2 + z_lo), core: 2. Of those that a mesh axis runs over, the one named last changes fastest.
Arguments:
- snapshots: bfloat16 [3, 12, 1536, 2048], P(None, None, 'span', 'snap'), may hold values from -12 to 12
Outputs:
- gram: float32 [2048, 2048], P('snap', 'span')
- mirror_gram: float32 [2048, 2048], P('snap', 'span')
The draws below stay inside these ranges and needn't reach their ends.
All inputs are finite; a program needn't handle non-finite values.
Results may differ from the reference program's by a relative error of at most 0.0003.
Values may be sent and summed in bfloat16 or wider, within the bound.
No kernel may reach another device: no remote copies, remote signals or barrier semaphores. Data moves between devices by JAX's collectives and lax.ppermute only.
A program may use at most 128 MiB of HBM per device.

```python
import math
import jax
import jax.numpy as jnp
from jax import lax

NZ = 1536
NXW = 12
SNAPS = 2048


def draw_snapshots(key, part):
    key = jax.random.fold_in(key, 11)
    key_amp, key_noise = jax.random.split(key, 2)
    amplitude = jnp.exp(jax.random.uniform(key_amp, (SNAPS,), jnp.float32, math.log(0.3), math.log(3.0)))
    weights = jnp.array([1.0, 0.7, 0.8], jnp.float32).reshape(3, 1, 1, 1)
    shape = (3, NXW, NZ, SNAPS)
    field = jnp.clip(jax.random.normal(key_noise, shape, jnp.float32), -4.0, 4.0)
    return (field * weights * amplitude).astype(jnp.bfloat16)


def setup_inputs(seed: int = 0) -> dict:
    arg_keys = jax.random.split(jax.random.key(seed), 2)
    return {
        "snapshots": draw_snapshots(jax.random.fold_in(arg_keys[1], 71), 0),
    }


def reference(snapshots):
    sign = jnp.array([1.0, 1.0, -1.0], jnp.float32).reshape(3, 1, 1, 1)
    reflected = (jnp.flip(snapshots.astype(jnp.float32), 2) * sign).astype(jnp.bfloat16)
    flat = snapshots.astype(jnp.float32).reshape(-1, SNAPS)
    mirrored = reflected.astype(jnp.float32).reshape(-1, SNAPS)
    scale = 1.0 / (NXW * NZ)
    dims = (((0,), (0,)), ((), ()))
    gram = lax.dot_general(flat, flat, dims, precision=lax.Precision.HIGHEST, preferred_element_type=jnp.float32)
    mirror_gram = lax.dot_general(flat, mirrored, dims, precision=lax.Precision.HIGHEST, preferred_element_type=jnp.float32)
    return gram * scale, mirror_gram * scale
```

```python
import functools

import jax
import jax.numpy as jnp
from jax import lax
from jax.sharding import PartitionSpec as P

NZ = 1536
NXW = 12
AXES = ("snap", "span")
COORDS = [
    (x, h, c, y, l)
    for x in range(4) for h in range(2) for c in range(2) for y in range(4) for l in range(2)
]


def place(x, h, c, y, l):
    return (x % 4 * 4 + h * 2 + c) * 8 + y % 4 * 2 + l


def send(value, target):
    pairs = []
    for at in COORDS:
        to = target(*at)
        if to is not None:
            pairs.append((place(*at), place(*to)))
    return lax.ppermute(value, AXES, pairs)


def inner(left, right):
    return lax.dot_general(
        left, right, (((0,), (0,)), ((), ())), preferred_element_type=jnp.float32
    )


def body(snapshots):
    comps, rows, depth, own = snapshots.shape
    quarter = rows // 4
    count = comps * quarter * depth
    snap, span = lax.axis_index("snap"), lax.axis_index("span")
    x, h, c = snap // 4, snap // 2 % 2, snap % 2
    y, l = span // 2, span % 2
    m = y // 2

    def part(side, group):
        return lax.dynamic_slice_in_dim(snapshots, (side * 2 + group) * quarter, quarter, axis=1)

    sign = jnp.array([1.0, 1.0, -1.0], jnp.bfloat16).reshape(3, 1, 1, 1)
    swap = jnp.flip(jnp.eye(depth, dtype=jnp.bfloat16), 0)

    def reflect(piece):
        turned = lax.dot_general(piece, swap, (((2,), (1,)), ((), ())), preferred_element_type=jnp.bfloat16)
        return jnp.swapaxes(turned, 2, 3) * sign

    flat = lambda piece: piece.reshape(count, own)

    with jax.named_scope("rows"):
        s0 = flat(part(m, h))
        t0 = send(flat(reflect(part(1 - m, h))), lambda x, h, c, y, l: (x, h, c, 3 - y, 1 - l))
        s1 = send(flat(part(m, 1 - h)), lambda x, h, c, y, l: (x, 1 - h, c, y, l))
        t1 = send(flat(reflect(part(1 - m, 1 - h))), lambda x, h, c, y, l: (x, 1 - h, c, 3 - y, 1 - l))

    pieces = (s0, t0, s1, t1)
    with jax.named_scope("cores"):
        other = [send(p, lambda x, h, c, y, l: (x, h, 1 - c, y, l)) for p in pieces]
        left_s = jnp.concatenate([s0, s1, other[0], other[2]], axis=1)
        left_t = jnp.concatenate([t0, t1, other[1], other[3]], axis=1)
        left = jnp.concatenate([left_s, left_t], axis=0)

    with jax.named_scope("next"):
        one = [send(p, lambda x, h, c, y, l: (x - 1, h, c, y, l)) for p in pieces]
    with jax.named_scope("opposite"):
        half = count // 2
        two = []
        for q in range(2):
            pair = jnp.stack(
                [lax.dynamic_slice_in_dim(p, (1 - x // 2) * half, half, axis=0) for p in pieces[2 * q:2 * q + 2]]
            )
            pair = send(pair, lambda x, h, c, y, l: (x + 1, h, c, y, l))
            pair = send(pair, lambda x, h, c, y, l: (x + 1, h, c, y, l))
            two += [pair[0], pair[1]]
        mine = (x // 2) * half
        left_half = jnp.concatenate(
            [
                lax.dynamic_slice_in_dim(left_s, mine, half, axis=0),
                lax.dynamic_slice_in_dim(left_t, mine, half, axis=0),
            ],
            axis=0,
        )

    def products(lhs, s, t):
        right = jnp.concatenate(
            [jnp.concatenate([s, t], axis=1), jnp.concatenate([t, s], axis=1)], axis=0
        )
        return inner(lhs, right).reshape(2, 2, own, 2 * own)

    def over_z(first, second):
        both = jnp.stack([first, second])

        def block(k):
            to = (2 * h + l + k) % 4
            piece = lax.dynamic_index_in_dim(both, (to % 2) ^ h, 0, keepdims=False)
            return lax.dynamic_index_in_dim(piece, (to // 2) ^ h, 1, keepdims=False)

        total = block(0)
        for k in (1, 2, 3):
            def target(x, h, c, y, l, k=k):
                to = (2 * h + l + k) % 4
                return (x, to // 2, c, y, to % 2)
            total = total + send(block(k), target)
        return total

    with jax.named_scope("blocks"):
        summed = [
            over_z(products(left, s0, t0), products(left, s1, t1)),
            over_z(products(left, one[0], one[1]), products(left, one[2], one[3])),
            over_z(products(left_half, two[0], two[1]), products(left_half, two[2], two[3])),
        ]

    with jax.named_scope("over_y"):
        stacked = jnp.stack(summed + [jnp.zeros_like(summed[0])])
        pick = lambda k: lax.dynamic_index_in_dim(stacked, (y + k - x) % 4, 0, keepdims=False)
        total = pick(0)
        for k in (1, 2, 3):
            def target(x, h, c, y, l, k=k):
                return (x, h, c, y + k, l) if (y + k - x) % 4 < 3 else None
            total = total + send(pick(k), target)
        total = total * (1.0 / (NXW * NZ))

    with jax.named_scope("place"):
        total = total.reshape(2, own, 2, own)
        received = send(total[1], lambda x, h, c, y, l: (x, h, 1 - c, y, l))
        straight = jnp.where(
            c == 0,
            jnp.stack([total[0], received], axis=2),
            jnp.stack([received, total[0]], axis=2),
        )
        straight = straight.transpose(1, 0, 2, 3).reshape(2, own, 2 * own)
        by_core = jnp.where(c == 0, total, total[::-1])
        turned = by_core.transpose(2, 3, 0, 1).reshape(2, own, 2 * own)

        def transposed(x, h, c, y, l):
            return (y, l, c, x, h) if (y - x) % 4 in (1, 2) else None

        turned = send(turned, transposed)
        d = (y - x) % 4
        result = jnp.where(d == 3, turned, jnp.where(d == 2, straight + turned, straight))
    return result[0], result[1]


def solution(mesh):
    placed = (P(None, None, "span", "snap"),)
    return jax.shard_map(
        body,
        mesh=mesh,
        in_specs=placed,
        out_specs=(P("snap", "span"), P("snap", "span")),
        check_vma=False,
    )
```

```python
import functools

import jax
import jax.numpy as jnp
from jax import lax
from jax.sharding import PartitionSpec as P

NZ = 1536
NXW = 12
AXES = ("snap", "span")
SWAPS = ((), (2, 3), (0,))
COORDS = [
    (x, h, c, y, l)
    for x in range(4) for h in range(2) for c in range(2) for y in range(4) for l in range(2)
]


def place(x, h, c, y, l):
    return (x % 4 * 4 + h * 2 + c) * 8 + y % 4 * 2 + l


def after(value, *others):
    return lax.optimization_barrier((value, *others))[0]


def send(value, target, behind=()):
    if behind:
        value = after(value, *behind)
    pairs = []
    for at in COORDS:
        to = target(*at)
        if to is not None:
            pairs.append((place(*at), place(*to)))
    return lax.ppermute(value, AXES, pairs)


def inner(left, right):
    return lax.dot_general(
        left, right, (((0,), (0,)), ((), ())), preferred_element_type=jnp.float32
    )


def up(x, h, c, y, l):
    return x + 1, h, c, y, l


def down(x, h, c, y, l):
    return x - 1, h, c, y, l


def across(x, h, c, y, l):
    return x, h, 1 - c, y, l


def body(snapshots):
    comps, rows, depth, own = snapshots.shape
    quarter = rows // 4
    count = comps * quarter * depth
    snap, span = lax.axis_index("snap"), lax.axis_index("span")
    x, h, c = snap // 4, snap // 2 % 2, snap % 2
    y, l = span // 2, span % 2
    m = y // 2

    def part(side, group):
        return lax.dynamic_slice_in_dim(snapshots, (side * 2 + group) * quarter, quarter, axis=1)

    sign = jnp.array([1.0, 1.0, -1.0], jnp.bfloat16).reshape(3, 1, 1, 1)
    swap = jnp.flip(jnp.eye(depth, dtype=jnp.bfloat16), 0)

    def reflect(piece):
        turned = lax.dot_general(piece, swap, (((2,), (1,)), ((), ())), preferred_element_type=jnp.bfloat16)
        return jnp.swapaxes(turned, 2, 3) * sign

    flat = lambda piece: piece.reshape(count, own)
    def above(x, h, c, y, l):
        return (x + 1, h, c, y, l) if (y - x - 1) % 4 < 2 else None

    with jax.named_scope("rows"):
        s1 = send(flat(part(m, 1 - h)), lambda x, h, c, y, l: (x, 1 - h, c, y, l))
        t0 = send(flat(reflect(part(1 - m, h))), lambda x, h, c, y, l: (x, h, c, 3 - y, 1 - l))
        crossing = flat(reflect(part(1 - m, 1 - h)))
        t1 = send(crossing, lambda x, h, c, y, l: (x, 1 - h, c, 3 - y, 1 - l))
        s0 = flat(part(m, h))
    with jax.named_scope("first"):
        n0 = send(s0, down)
        p0 = send(s0, above)
        n1 = send(t0, down, [n0])
        p1 = send(t0, above, [p0])
    with jax.named_scope("second"):
        pair = jnp.concatenate([s1, t1])
        n2 = send(pair, down)
        p2 = send(pair, above)
        c0, c1, c2 = send(s0, across, [s1, t1, n1, p1]), send(t0, across, [s1, t1, n1, p1]), send(pair, across)
        s0, t0, n1, p0, p1 = after((s0, t0, n1, p0, p1), c0, c1, c2)
        q0, q1 = send(p0, across), send(p1, across)
        p0, p1 = after((p0, p1), q0, q1)

    def columns(name, *cores):
        with jax.named_scope(name):
            result = jnp.zeros((2 * count, 4 * own), jnp.bfloat16)
            for i, (s, t, st) in enumerate(cores):
                result = lax.dynamic_update_slice(result, s, (0, 2 * i * own))
                result = lax.dynamic_update_slice(result, t, (count, 2 * i * own))
                result = lax.dynamic_update_slice(result, st[:count], (0, (2 * i + 1) * own))
                result = lax.dynamic_update_slice(result, st[count:], (count, (2 * i + 1) * own))
            return result

    left = columns("left", (s0, t0, pair), (c0, c1, c2))

    def products(lhs, s, t):
        right = jnp.concatenate(
            [jnp.concatenate([s, t], axis=1), jnp.concatenate([t, s], axis=1)], axis=0
        )
        return inner(lhs, right).reshape(2, 2, own, 2 * own)

    d = (y - x) % 4

    def over_z(first, second, behind, active=lambda *at: True, swaps=()):
        swap = functools.reduce(jnp.logical_or, [d == at for at in swaps], jnp.zeros((), bool))

        def block(k):
            to = (2 * h + l + k) % 4
            row, column = jnp.where(swap, to % 2, to // 2), jnp.where(swap, to // 2, to % 2)
            pick = lambda both: lax.dynamic_index_in_dim(both, row ^ h, 1, keepdims=False)
            return jnp.where(column ^ h == 0, pick(first), pick(second))

        total = block(0)
        for k in (1, 2, 3):
            def target(x, h, c, y, l, k=k):
                to = (2 * h + l + k) % 4
                return (x, to // 2, c, y, to % 2) if active(x, h, c, y, l) else None
            total = total + send(block(k), target, behind)
        return total

    with jax.named_scope("same"):
        same = over_z(products(left, s0, t0), products(left, pair[:count], pair[count:]), [q0, q1])
    with jax.named_scope("beside"):
        n2 = after(n2, same)
        beside = over_z(products(left, n0, n1), products(left, n2[:count], n2[count:]), [], swaps=SWAPS[1])
    with jax.named_scope("around"):
        p2 = after(p2, same)
        q2 = send(p2, across)
        previous = columns("previous", (p0, p1, p2), (q0, q1, q2))
        around = over_z(
            products(previous, n0, n1),
            products(previous, n2[:count], n2[count:]),
            [],
            lambda x, h, c, y, l: (y - x) % 4 < 2,
            SWAPS[2],
        )

    rounds = (
        ((1, True), (2, False), (1, False), (0, False)),
        ((1, False), (2, True), (0, False), (1, True)),
        ((2, False), (0, False), (1, True), (1, False)),
        ((2, True), (1, True), None, None),
    )
    with jax.named_scope("over_y"):
        got = []
        for plan in rounds:
            def target(x, h, c, y, l, plan=plan):
                if plan[(y - x) % 4] is None:
                    return None
                block, turn = plan[(y - x) % 4]
                row, column = ((x, x), (x, x + 1), (x - 1, x + 1))[block]
                if turn:
                    row, column = column, row
                if turn != ((y - x) % 4 in SWAPS[block]):
                    h, l = l, h
                return row % 4, h, c, column, l
            value = beside
            for at, step in enumerate(plan):
                if step is not None and step[0] != 1:
                    value = jnp.where(d == at, (same, beside, around)[step[0]], value)
            got.append(send(value, target))
        own_block = jnp.where(d == 0, same, beside)
        odd = got[0] + got[2]
        straight = odd + jnp.where(d == 2, 0, own_block + got[1])
        turned = jnp.where(d == 2, 0, odd) + got[1] + got[3]

    with jax.named_scope("place"):
        scale = 1.0 / (NXW * NZ)
        total = (straight * scale).reshape(2, own, 2, own)
        turned = (turned * scale).reshape(2, own, 2, own)
        received = send(total[1], across)
        straight = jnp.where(
            c == 0,
            jnp.stack([total[0], received], axis=2),
            jnp.stack([received, total[0]], axis=2),
        )
        straight = straight.transpose(1, 0, 2, 3).reshape(2, own, 2 * own)
        by_core = jnp.where(c == 0, turned, turned[::-1])
        turned = by_core.transpose(2, 3, 0, 1).reshape(2, own, 2 * own)
        result = jnp.where(d == 3, turned, jnp.where(d == 2, straight + turned, straight))
    return result[0], result[1]


def solution(mesh):
    placed = (P(None, None, "span", "snap"),)
    return jax.shard_map(
        body,
        mesh=mesh,
        in_specs=placed,
        out_specs=(P("snap", "span"), P("snap", "span")),
        check_vma=False,
    )
```

```python
import functools

import jax
import jax.numpy as jnp
from jax import lax
from jax.sharding import PartitionSpec as P

NZ = 1536
NXW = 12
AXES = ("snap", "span")
SWAPS = ((), (2, 3), (0,))
COORDS = [
    (x, h, c, y, l)
    for x in range(4) for h in range(2) for c in range(2) for y in range(4) for l in range(2)
]


def place(x, h, c, y, l):
    return (x % 4 * 4 + h * 2 + c) * 8 + y % 4 * 2 + l


def after(value, *others):
    return lax.optimization_barrier((value, *others))[0]


def send(value, target, behind=()):
    if behind:
        value = after(value, *behind)
    pairs = []
    for at in COORDS:
        to = target(*at)
        if to is not None:
            pairs.append((place(*at), place(*to)))
    return lax.ppermute(value, AXES, pairs)


def inner(left, right):
    return lax.dot_general(
        left, right, (((0,), (0,)), ((), ())), preferred_element_type=jnp.float32
    )


def up(x, h, c, y, l):
    return x + 1, h, c, y, l


def down(x, h, c, y, l):
    return x - 1, h, c, y, l


def across(x, h, c, y, l):
    return x, h, 1 - c, y, l


def body(snapshots):
    comps, rows, depth, own = snapshots.shape
    quarter = rows // 4
    count = comps * quarter * depth
    snap, span = lax.axis_index("snap"), lax.axis_index("span")
    x, h, c = snap // 4, snap // 2 % 2, snap % 2
    y, l = span // 2, span % 2
    m = y // 2

    def part(side, group):
        return lax.dynamic_slice_in_dim(snapshots, (side * 2 + group) * quarter, quarter, axis=1)

    sign = jnp.array([1.0, 1.0, -1.0], jnp.bfloat16).reshape(3, 1, 1, 1)
    swap = jnp.flip(jnp.eye(depth, dtype=jnp.bfloat16), 0)

    def reflect(piece):
        turned = lax.dot_general(piece, swap, (((2,), (1,)), ((), ())), preferred_element_type=jnp.bfloat16)
        return jnp.swapaxes(turned, 2, 3) * sign

    flat = lambda piece: piece.reshape(count, own)
    def above(x, h, c, y, l):
        return (x + 1, h, c, y, l) if (y - x - 1) % 4 < 2 else None

    with jax.named_scope("rows"):
        s1 = flat(send(part(m, 1 - h), lambda x, h, c, y, l: (x, 1 - h, c, y, l)))
        t0 = send(part(1 - m, h), lambda x, h, c, y, l: (x, h, c, 3 - y, 1 - l))
        t1 = send(part(1 - m, 1 - h), lambda x, h, c, y, l: (x, 1 - h, c, 3 - y, 1 - l))
        t0, t1 = flat(reflect(t0)), flat(reflect(t1))
        s0 = after(flat(part(m, h)), swap)
    with jax.named_scope("first"):
        n0 = send(s0, down)
        p0 = send(s0, above)
        n1 = send(t0, down, [n0])
        p1 = send(t0, above, [p0])
    with jax.named_scope("second"):
        pair = jnp.concatenate([s1, t1])
        n2 = send(pair, down)
        p2 = send(pair, above)
        c0, c1, c2 = send(s0, across, [s1, t1, n1, p1]), send(t0, across, [s1, t1, n1, p1]), send(pair, across)
        s0, t0, n1, p0, p1 = after((s0, t0, n1, p0, p1), c0, c1, c2)
        q0, q1 = send(p0, across), send(p1, across)
        p0, p1 = after((p0, p1), q0, q1)

    def columns(name, *cores):
        with jax.named_scope(name):
            result = jnp.zeros((2 * count, 4 * own), jnp.bfloat16)
            for i, (s, t, st) in enumerate(cores):
                result = lax.dynamic_update_slice(result, s, (0, 2 * i * own))
                result = lax.dynamic_update_slice(result, t, (count, 2 * i * own))
                result = lax.dynamic_update_slice(result, st[:count], (0, (2 * i + 1) * own))
                result = lax.dynamic_update_slice(result, st[count:], (count, (2 * i + 1) * own))
            return result

    left = columns("left", (s0, t0, pair), (c0, c1, c2))

    def products(lhs, s, t):
        right = jnp.concatenate(
            [jnp.concatenate([s, t], axis=1), jnp.concatenate([t, s], axis=1)], axis=0
        )
        return inner(lhs, right).reshape(2, 2, own, 2 * own)

    d = (y - x) % 4

    def over_z(first, second, behind, active=lambda *at: True, swaps=()):
        swap = functools.reduce(jnp.logical_or, [d == at for at in swaps], jnp.zeros((), bool))

        def block(k):
            to = (2 * h + l + k) % 4
            row, column = jnp.where(swap, to % 2, to // 2), jnp.where(swap, to // 2, to % 2)
            pick = lambda both: lax.dynamic_index_in_dim(both, row ^ h, 1, keepdims=False)
            return jnp.where(column ^ h == 0, pick(first), pick(second))

        total = block(0)
        for k in (3, 1, 2):
            def target(x, h, c, y, l, k=k):
                to = (2 * h + l + k) % 4
                return (x, to // 2, c, y, to % 2) if active(x, h, c, y, l) else None
            total = total + send(block(k), target, behind)
        return total

    with jax.named_scope("same"):
        same = over_z(products(left, s0, t0), products(left, pair[:count], pair[count:]), [])
    with jax.named_scope("beside"):
        n2 = after(n2, same)
        beside = over_z(products(left, n0, n1), products(left, n2[:count], n2[count:]), [], swaps=SWAPS[1])
    with jax.named_scope("around"):
        p2 = after(p2, same)
        q2 = send(p2, across)
        previous = columns("previous", (p0, p1, p2), (q0, q1, q2))
        around = over_z(
            products(previous, n0, n1),
            products(previous, n2[:count], n2[count:]),
            [],
            lambda x, h, c, y, l: (y - x) % 4 < 2,
            SWAPS[2],
        )

    same, beside = lax.optimization_barrier((same, beside))

    rounds = (
        ((1, True), (2, False), (1, False), (0, False)),
        ((1, False), (2, True), (0, False), (1, True)),
        ((2, False), (0, False), (1, True), (1, False)),
        ((2, True), (1, True), None, None),
    )
    with jax.named_scope("over_y"):
        got = []
        for plan in rounds:
            def target(x, h, c, y, l, plan=plan):
                if plan[(y - x) % 4] is None:
                    return None
                block, turn = plan[(y - x) % 4]
                row, column = ((x, x), (x, x + 1), (x - 1, x + 1))[block]
                if turn:
                    row, column = column, row
                if turn != ((y - x) % 4 in SWAPS[block]):
                    h, l = l, h
                return row % 4, h, c, column, l
            value = beside
            for at, step in enumerate(plan):
                if step is not None and step[0] != 1:
                    value = jnp.where(d == at, (same, beside, around)[step[0]], value)
            got.append(send(value, target))
        own_block = jnp.where(d == 0, same, beside)
        odd = got[0] + got[2]
        straight = odd + jnp.where(d == 2, 0, own_block + got[1])
        turned = jnp.where(d == 2, 0, odd) + got[1] + got[3]

    with jax.named_scope("place"):
        scale = 1.0 / (NXW * NZ)
        total = (straight * scale).reshape(2, own, 2, own)
        turned = (turned * scale).reshape(2, own, 2, own)
        received = send(total[1], across)
        straight = jnp.where(
            c == 0,
            jnp.stack([total[0], received], axis=2),
            jnp.stack([received, total[0]], axis=2),
        )
        straight = straight.transpose(1, 0, 2, 3).reshape(2, own, 2 * own)
        by_core = jnp.where(c == 0, turned, turned[::-1])
        turned = by_core.transpose(2, 3, 0, 1).reshape(2, own, 2 * own)
        result = jnp.where(d == 3, turned, jnp.where(d == 2, straight + turned, straight))
    return result[0], result[1]


def solution(mesh):
    placed = (P(None, None, "span", "snap"),)
    return jax.shard_map(
        body,
        mesh=mesh,
        in_specs=placed,
        out_specs=(P("snap", "span"), P("snap", "span")),
        check_vma=False,
    )
```

```python
import functools

import jax
import jax.numpy as jnp
from jax import lax
from jax.sharding import PartitionSpec as P

NZ = 1536
NXW = 12
AXES = ("snap", "span")
SWAPS = ((), (2, 3), (0,))
COORDS = [
    (x, h, c, y, l)
    for x in range(4) for h in range(2) for c in range(2) for y in range(4) for l in range(2)
]


def place(x, h, c, y, l):
    return (x % 4 * 4 + h * 2 + c) * 8 + y % 4 * 2 + l


def after(value, *others):
    return lax.optimization_barrier((value, *others))[0]


def send(value, target, behind=()):
    if behind:
        value = after(value, *behind)
    pairs = []
    for at in COORDS:
        to = target(*at)
        if to is not None:
            pairs.append((place(*at), place(*to)))
    return lax.ppermute(value, AXES, pairs)


def inner(left, right):
    return lax.dot_general(
        left, right, (((0,), (0,)), ((), ())), preferred_element_type=jnp.float32
    )


def up(x, h, c, y, l):
    return x + 1, h, c, y, l


def down(x, h, c, y, l):
    return x - 1, h, c, y, l


def across(x, h, c, y, l):
    return x, h, 1 - c, y, l


def body(snapshots):
    comps, rows, depth, own = snapshots.shape
    quarter = rows // 4
    count = comps * quarter * depth
    snap, span = lax.axis_index("snap"), lax.axis_index("span")
    x, h, c = snap // 4, snap // 2 % 2, snap % 2
    y, l = span // 2, span % 2
    m = y // 2

    def part(side, group):
        return lax.dynamic_slice_in_dim(snapshots, (side * 2 + group) * quarter, quarter, axis=1)

    sign = jnp.array([1.0, 1.0, -1.0], jnp.bfloat16).reshape(3, 1, 1, 1)
    swap = jnp.flip(jnp.eye(depth, dtype=jnp.bfloat16), 0)

    def reflect(piece):
        turned = lax.dot_general(piece, swap, (((2,), (1,)), ((), ())), preferred_element_type=jnp.bfloat16)
        return jnp.swapaxes(turned, 2, 3) * sign

    flat = lambda piece: piece.reshape(count, own)
    def above(x, h, c, y, l):
        return (x + 1, h, c, y, l) if (y - x - 1) % 4 < 2 else None

    with jax.named_scope("rows"):
        s1 = flat(send(part(m, 1 - h), lambda x, h, c, y, l: (x, 1 - h, c, y, l)))
        t0 = send(part(1 - m, h), lambda x, h, c, y, l: (x, h, c, 3 - y, 1 - l))
        t1 = send(part(1 - m, 1 - h), lambda x, h, c, y, l: (x, 1 - h, c, 3 - y, 1 - l))
        t0, t1 = flat(reflect(t0)), flat(reflect(t1))
        s0 = after(flat(part(m, h)), swap)
    with jax.named_scope("first"):
        n0 = send(s0, down)
        p0 = send(s0, above)
        n1 = send(t0, down, [n0])
        p1 = send(t0, above, [p0])
    with jax.named_scope("second"):
        pair = jnp.concatenate([s1, t1])
        n2 = send(pair, down)
        p2 = send(pair, above)
        c0, c1, c2 = send(s0, across, [s1, t1, n1, p1]), send(t0, across, [s1, t1, n1, p1]), send(pair, across)
        s0, t0, n1, p0, p1 = after((s0, t0, n1, p0, p1), c0, c1, c2)
        q0, q1 = send(p0, across), send(p1, across)
        p0, p1 = after((p0, p1), q0, q1)

    def columns(name, *cores):
        with jax.named_scope(name):
            result = jnp.zeros((2 * count, 4 * own), jnp.bfloat16)
            for i, (s, t, st) in enumerate(cores):
                result = lax.dynamic_update_slice(result, s, (0, 2 * i * own))
                result = lax.dynamic_update_slice(result, t, (count, 2 * i * own))
                result = lax.dynamic_update_slice(result, st[:count], (0, (2 * i + 1) * own))
                result = lax.dynamic_update_slice(result, st[count:], (count, (2 * i + 1) * own))
            return result

    left = columns("left", (s0, t0, pair), (c0, c1, c2))

    def products(lhs, s, t):
        right = jnp.concatenate(
            [jnp.concatenate([s, t], axis=1), jnp.concatenate([t, s], axis=1)], axis=0
        )
        return inner(lhs, right).reshape(2, 2, own, 2 * own)

    d = (y - x) % 4

    def over_z(first, second, behind, active=lambda *at: True, swaps=()):
        swap = functools.reduce(jnp.logical_or, [d == at for at in swaps], jnp.zeros((), bool))

        def block(k):
            to = (2 * h + l + k) % 4
            row, column = jnp.where(swap, to % 2, to // 2), jnp.where(swap, to // 2, to % 2)
            pick = lambda both: lax.dynamic_index_in_dim(both, row ^ h, 1, keepdims=False)
            return jnp.where(column ^ h == 0, pick(first), pick(second))

        total = block(0)
        for k in (1, 3, 2):
            def target(x, h, c, y, l, k=k):
                to = (2 * h + l + k) % 4
                return (x, to // 2, c, y, to % 2) if active(x, h, c, y, l) else None
            total = total + send(block(k), target, behind)
        return total

    with jax.named_scope("same"):
        same = over_z(products(left, s0, t0), products(left, pair[:count], pair[count:]), [])
    with jax.named_scope("beside"):
        n2 = after(n2, same)
        beside = over_z(products(left, n0, n1), products(left, n2[:count], n2[count:]), [], swaps=SWAPS[1])
    with jax.named_scope("around"):
        p2 = after(p2, same)
        q2 = send(p2, across)
        previous = columns("previous", (p0, p1, p2), (q0, q1, q2))
        around = over_z(
            products(previous, n0, n1),
            products(previous, n2[:count], n2[count:]),
            [],
            lambda x, h, c, y, l: (y - x) % 4 < 2,
            SWAPS[2],
        )

    same, beside = lax.optimization_barrier((same, beside))

    rounds = (
        ((1, True), (2, False), (1, False), (0, False)),
        ((1, False), (2, True), (0, False), (1, True)),
        ((2, False), (0, False), (1, True), (1, False)),
        ((2, True), (1, True), None, None),
    )
    with jax.named_scope("over_y"):
        got = []
        for plan in rounds:
            def target(x, h, c, y, l, plan=plan):
                if plan[(y - x) % 4] is None:
                    return None
                block, turn = plan[(y - x) % 4]
                row, column = ((x, x), (x, x + 1), (x - 1, x + 1))[block]
                if turn:
                    row, column = column, row
                if turn != ((y - x) % 4 in SWAPS[block]):
                    h, l = l, h
                return row % 4, h, c, column, l
            value = beside
            for at, step in enumerate(plan):
                if step is not None and step[0] != 1:
                    value = jnp.where(d == at, (same, beside, around)[step[0]], value)
            got.append(send(value, target))
        own_block = jnp.where(d == 0, same, beside)
        odd = got[0] + got[2]
        straight = odd + jnp.where(d == 2, 0, own_block + got[1])
        turned = jnp.where(d == 2, 0, odd) + got[1] + got[3]

    with jax.named_scope("place"):
        scale = 1.0 / (NXW * NZ)
        mine, theirs = straight[0] * scale, straight[1] * scale
        received = send(theirs, across)
        turned = turned * scale
        first, second = jnp.where(c == 0, turned[0], turned[1]), jnp.where(c == 0, turned[1], turned[0])
        result = []
        for part in (slice(0, own), slice(own, 2 * own)):
            across_cores = jnp.concatenate([first[:, part].T, second[:, part].T], axis=1)
            lower, upper = mine[:, part], received[:, part]
            along = jnp.concatenate([jnp.where(c == 0, lower, upper), jnp.where(c == 0, upper, lower)], axis=1)
            result.append(jnp.where(d == 3, across_cores, jnp.where(d == 2, along + across_cores, along)))
    return result[0], result[1]


def solution(mesh):
    placed = (P(None, None, "span", "snap"),)
    return jax.shard_map(
        body,
        mesh=mesh,
        in_specs=placed,
        out_specs=(P("snap", "span"), P("snap", "span")),
        check_vma=False,
    )
```

```python
import functools

import jax
import jax.numpy as jnp
from jax import lax
from jax.sharding import PartitionSpec as P

NZ = 1536
NXW = 12
AXES = ("snap", "span")
SWAPS = ((), (2, 3), (0,))
COORDS = [
    (x, h, c, y, l)
    for x in range(4) for h in range(2) for c in range(2) for y in range(4) for l in range(2)
]


def place(x, h, c, y, l):
    return (x % 4 * 4 + h * 2 + c) * 8 + y % 4 * 2 + l


def after(value, *others):
    return lax.optimization_barrier((value, *others))[0]


def send(value, target, behind=()):
    if behind:
        value = after(value, *behind)
    pairs = []
    for at in COORDS:
        to = target(*at)
        if to is not None:
            pairs.append((place(*at), place(*to)))
    return lax.ppermute(value, AXES, pairs)


def inner(left, right):
    return lax.dot_general(
        left, right, (((0,), (0,)), ((), ())), preferred_element_type=jnp.float32
    )


def up(x, h, c, y, l):
    return x + 1, h, c, y, l


def down(x, h, c, y, l):
    return x - 1, h, c, y, l


def across(x, h, c, y, l):
    return x, h, 1 - c, y, l


def body(snapshots):
    comps, rows, depth, own = snapshots.shape
    quarter = rows // 4
    count = comps * quarter * depth
    snap, span = lax.axis_index("snap"), lax.axis_index("span")
    x, h, c = snap // 4, snap // 2 % 2, snap % 2
    y, l = span // 2, span % 2
    m = y // 2

    def part(side, group):
        return lax.dynamic_slice_in_dim(snapshots, (side * 2 + group) * quarter, quarter, axis=1)

    sign = jnp.array([1.0, 1.0, -1.0], jnp.bfloat16).reshape(3, 1, 1, 1)
    swap = jnp.flip(jnp.eye(depth, dtype=jnp.bfloat16), 0)

    def reflect(piece):
        turned = lax.dot_general(piece, swap, (((2,), (1,)), ((), ())), preferred_element_type=jnp.bfloat16)
        return jnp.swapaxes(turned, 2, 3) * sign

    flat = lambda piece: piece.reshape(count, own)
    def above(x, h, c, y, l):
        return (x + 1, h, c, y, l) if (y - x - 1) % 4 < 2 else None

    with jax.named_scope("rows"):
        s1 = flat(send(part(m, 1 - h), lambda x, h, c, y, l: (x, 1 - h, c, y, l)))
        t0 = send(part(1 - m, h), lambda x, h, c, y, l: (x, h, c, 3 - y, 1 - l))
        t1 = send(part(1 - m, 1 - h), lambda x, h, c, y, l: (x, 1 - h, c, 3 - y, 1 - l))
        t0, t1 = flat(reflect(t0)), flat(reflect(t1))
        s0 = after(flat(part(m, h)), swap)
    with jax.named_scope("first"):
        n0 = send(s0, down)
        p0 = send(s0, above)
        n1 = send(t0, down, [n0])
        p1 = send(t0, above, [p0])
    with jax.named_scope("second"):
        pair = jnp.concatenate([s1, t1])
        n2 = send(pair, down)
        p2 = send(pair, above)
        c0, c1, c2 = send(s0, across, [s1, t1, n1, p1]), send(t0, across, [s1, t1, n1, p1]), send(pair, across)
        s0, t0, n1, p0, p1 = after((s0, t0, n1, p0, p1), c0, c1, c2)
        q0, q1 = send(p0, across), send(p1, across)
        p0, p1 = after((p0, p1), q0, q1)

    def columns(name, *cores):
        with jax.named_scope(name):
            result = jnp.zeros((2 * count, 4 * own), jnp.bfloat16)
            for i, (s, t, st) in enumerate(cores):
                result = lax.dynamic_update_slice(result, s, (0, 2 * i * own))
                result = lax.dynamic_update_slice(result, t, (count, 2 * i * own))
                result = lax.dynamic_update_slice(result, st[:count], (0, (2 * i + 1) * own))
                result = lax.dynamic_update_slice(result, st[count:], (count, (2 * i + 1) * own))
            return result

    left = columns("left", (s0, t0, pair), (c0, c1, c2))

    def products(lhs, s, t):
        right = jnp.concatenate(
            [jnp.concatenate([s, t], axis=1), jnp.concatenate([t, s], axis=1)], axis=0
        )
        return inner(lhs, right).reshape(2, 2, own, 2 * own)

    d = (y - x) % 4

    def over_z(first, second, behind, active=lambda *at: True, swaps=()):
        swap = functools.reduce(jnp.logical_or, [d == at for at in swaps], jnp.zeros((), bool))

        def block(k):
            to = (2 * h + l + k) % 4
            row, column = jnp.where(swap, to % 2, to // 2), jnp.where(swap, to // 2, to % 2)
            pick = lambda both: lax.dynamic_index_in_dim(both, row ^ h, 1, keepdims=False)
            return jnp.where(column ^ h == 0, pick(first), pick(second))

        total = block(0)
        for k in (1, 3, 2):
            def target(x, h, c, y, l, k=k):
                to = (2 * h + l + k) % 4
                return (x, to // 2, c, y, to % 2) if active(x, h, c, y, l) else None
            total = total + send(block(k), target, behind)
        return total

    with jax.named_scope("same"):
        same = over_z(products(left, s0, t0), products(left, pair[:count], pair[count:]), [])
    with jax.named_scope("beside"):
        n2 = after(n2, same)
        beside = over_z(products(left, n0, n1), products(left, n2[:count], n2[count:]), [], swaps=SWAPS[1])
    with jax.named_scope("around"):
        p2 = after(p2, same)
        q2 = send(p2, across)
        previous = columns("previous", (p0, p1, p2), (q0, q1, q2))
        around = over_z(
            products(previous, n0, n1),
            products(previous, n2[:count], n2[count:]),
            [],
            lambda x, h, c, y, l: (y - x) % 4 < 2,
            SWAPS[2],
        )

    same, beside = lax.optimization_barrier((same, beside))
    mixed = lax.optimization_barrier(tuple(jnp.where(d == at, same, beside) for at in (3, 2, 1)))

    rounds = (
        ((1, True), (2, False), (1, False), (0, False)),
        ((1, False), (2, True), (0, False), (1, True)),
        ((2, False), (0, False), (1, True), (1, False)),
        ((2, True), (1, True), None, None),
    )
    with jax.named_scope("over_y"):
        got = []
        for plan in rounds:
            def target(x, h, c, y, l, plan=plan):
                if plan[(y - x) % 4] is None:
                    return None
                block, turn = plan[(y - x) % 4]
                row, column = ((x, x), (x, x + 1), (x - 1, x + 1))[block]
                if turn:
                    row, column = column, row
                if turn != ((y - x) % 4 in SWAPS[block]):
                    h, l = l, h
                return row % 4, h, c, column, l
            value = (mixed + (beside,))[len(got)]
            for at, step in enumerate(plan):
                if step is not None and step[0] == 2:
                    value = jnp.where(d == at, around, value)
            got.append(send(value, target))
        own_block = jnp.where(d == 0, same, beside)
        odd = got[0] + got[2]
        straight = odd + jnp.where(d == 2, 0, own_block + got[1])
        turned = jnp.where(d == 2, 0, odd) + got[1] + got[3]

    with jax.named_scope("place"):
        scale = 1.0 / (NXW * NZ)
        mine, theirs = straight[0] * scale, straight[1] * scale
        received = send(theirs, across)
        turned = turned * scale
        first, second = jnp.where(c == 0, turned[0], turned[1]), jnp.where(c == 0, turned[1], turned[0])
        result = []
        for part in (slice(0, own), slice(own, 2 * own)):
            across_cores = jnp.concatenate([first[:, part].T, second[:, part].T], axis=1)
            lower, upper = mine[:, part], received[:, part]
            along = jnp.concatenate([jnp.where(c == 0, lower, upper), jnp.where(c == 0, upper, lower)], axis=1)
            result.append(jnp.where(d == 3, across_cores, jnp.where(d == 2, along + across_cores, along)))
    return result[0], result[1]


def solution(mesh):
    placed = (P(None, None, "span", "snap"),)
    return jax.shard_map(
        body,
        mesh=mesh,
        in_specs=placed,
        out_specs=(P("snap", "span"), P("snap", "span")),
        check_vma=False,
    )
```

```python
import functools

import jax
import jax.numpy as jnp
from jax import lax
from jax.sharding import PartitionSpec as P

NZ = 1536
NXW = 12
AXES = ("snap", "span")
SWAPS = ((), (2, 3), (0,))
COORDS = [
    (x, h, c, y, l)
    for x in range(4) for h in range(2) for c in range(2) for y in range(4) for l in range(2)
]


def place(x, h, c, y, l):
    return (x % 4 * 4 + h * 2 + c) * 8 + y % 4 * 2 + l


def after(value, *others):
    return lax.optimization_barrier((value, *others))[0]


def send(value, target, behind=()):
    if behind:
        value = after(value, *behind)
    pairs = []
    for at in COORDS:
        to = target(*at)
        if to is not None:
            pairs.append((place(*at), place(*to)))
    return lax.ppermute(value, AXES, pairs)


def inner(left, right):
    return lax.dot_general(
        left, right, (((0,), (0,)), ((), ())), preferred_element_type=jnp.float32
    )


def up(x, h, c, y, l):
    return x + 1, h, c, y, l


def down(x, h, c, y, l):
    return x - 1, h, c, y, l


def across(x, h, c, y, l):
    return x, h, 1 - c, y, l


def body(snapshots):
    comps, rows, depth, own = snapshots.shape
    quarter = rows // 4
    count = comps * quarter * depth
    snap, span = lax.axis_index("snap"), lax.axis_index("span")
    x, h, c = snap // 4, snap // 2 % 2, snap % 2
    y, l = span // 2, span % 2
    m = y // 2

    def part(side, group):
        return lax.dynamic_slice_in_dim(snapshots, (side * 2 + group) * quarter, quarter, axis=1)

    sign = jnp.array([1.0, 1.0, -1.0], jnp.bfloat16).reshape(3, 1, 1, 1)
    swap = jnp.flip(jnp.eye(depth, dtype=jnp.bfloat16), 0)

    def reflect(piece):
        turned = lax.dot_general(piece, swap, (((2,), (1,)), ((), ())), preferred_element_type=jnp.bfloat16)
        return jnp.swapaxes(turned, 2, 3) * sign

    flat = lambda piece: piece.reshape(count, own)
    def above(x, h, c, y, l):
        return (x + 1, h, c, y, l) if (y - x - 1) % 4 < 2 else None

    with jax.named_scope("rows"):
        s1 = flat(send(part(m, 1 - h), lambda x, h, c, y, l: (x, 1 - h, c, y, l)))
        t0 = send(part(1 - m, h), lambda x, h, c, y, l: (x, h, c, 3 - y, 1 - l))
        t1 = send(part(1 - m, 1 - h), lambda x, h, c, y, l: (x, 1 - h, c, 3 - y, 1 - l))
        t0, t1 = flat(reflect(t0)), flat(reflect(t1))
        s0 = after(flat(part(m, h)), swap)
    with jax.named_scope("first"):
        n0 = send(s0, down)
        p0 = send(s0, above)
        n1 = send(t0, down, [n0])
        p1 = send(t0, above, [p0])
    with jax.named_scope("second"):
        pair = jnp.concatenate([s1, t1])
        n2 = send(pair, down)
        p2 = send(pair, above)
        c0, c1, c2 = send(s0, across, [s1, t1, n1, p1]), send(t0, across, [s1, t1, n1, p1]), send(pair, across)
        s0, t0, n1, p0, p1 = after((s0, t0, n1, p0, p1), c0, c1, c2)
        q0, q1 = send(p0, across), send(p1, across)
        p0, p1 = after((p0, p1), q0, q1)

    def columns(name, *cores):
        with jax.named_scope(name):
            result = jnp.zeros((2 * count, 4 * own), jnp.bfloat16)
            for i, (s, t, st) in enumerate(cores):
                result = lax.dynamic_update_slice(result, s, (0, 2 * i * own))
                result = lax.dynamic_update_slice(result, t, (count, 2 * i * own))
                result = lax.dynamic_update_slice(result, st[:count], (0, (2 * i + 1) * own))
                result = lax.dynamic_update_slice(result, st[count:], (count, (2 * i + 1) * own))
            return result

    left = columns("left", (s0, t0, pair), (c0, c1, c2))

    def products(lhs, s, t):
        right = jnp.concatenate(
            [jnp.concatenate([s, t], axis=1), jnp.concatenate([t, s], axis=1)], axis=0
        )
        return inner(lhs, right).reshape(2, 2, own, 2 * own)

    def both_products(lhs, first, second):
        (s, t), (u, v) = first, second
        right = jnp.concatenate(
            [jnp.concatenate([s, t, u, v], axis=1), jnp.concatenate([t, s, v, u], axis=1)], axis=0
        )
        out = inner(lhs, right)
        return [out[:, q * 2 * own:(q + 1) * 2 * own].reshape(2, 2, own, 2 * own) for q in range(2)]

    d = (y - x) % 4

    def over_z(first, second, behind, active=lambda *at: True, swaps=()):
        swap = functools.reduce(jnp.logical_or, [d == at for at in swaps], jnp.zeros((), bool))

        def block(k):
            to = (2 * h + l + k) % 4
            row, column = jnp.where(swap, to % 2, to // 2), jnp.where(swap, to // 2, to % 2)
            pick = lambda both: lax.dynamic_index_in_dim(both, row ^ h, 1, keepdims=False)
            return jnp.where(column ^ h == 0, pick(first), pick(second))

        total = block(0)
        for k in (1, 3, 2):
            def target(x, h, c, y, l, k=k):
                to = (2 * h + l + k) % 4
                return (x, to // 2, c, y, to % 2) if active(x, h, c, y, l) else None
            total = total + send(block(k), target, behind)
        return total

    with jax.named_scope("same"):
        same = over_z(products(left, s0, t0), products(left, pair[:count], pair[count:]), [])
    with jax.named_scope("beside"):
        n2 = after(n2, same)
        beside = over_z(products(left, n0, n1), products(left, n2[:count], n2[count:]), [], swaps=SWAPS[1])
    with jax.named_scope("around"):
        p2 = after(p2, same)
        q2 = send(p2, across)
        previous = columns("previous", (p0, p1, p2), (q0, q1, q2))
        around = over_z(
            *both_products(previous, (n0, n1), (n2[:count], n2[count:])),
            [],
            lambda x, h, c, y, l: (y - x) % 4 < 2,
            SWAPS[2],
        )

    same, beside = lax.optimization_barrier((same, beside))
    mixed = lax.optimization_barrier(tuple(jnp.where(d == at, same, beside) for at in (3, 2, 1)))

    rounds = (
        ((1, True), (2, False), (1, False), (0, False)),
        ((1, False), (2, True), (0, False), (1, True)),
        ((2, False), (0, False), (1, True), (1, False)),
        ((2, True), (1, True), None, None),
    )
    with jax.named_scope("over_y"):
        got = []
        for plan in rounds:
            def target(x, h, c, y, l, plan=plan):
                if plan[(y - x) % 4] is None:
                    return None
                block, turn = plan[(y - x) % 4]
                row, column = ((x, x), (x, x + 1), (x - 1, x + 1))[block]
                if turn:
                    row, column = column, row
                if turn != ((y - x) % 4 in SWAPS[block]):
                    h, l = l, h
                return row % 4, h, c, column, l
            value = (mixed + (beside,))[len(got)]
            for at, step in enumerate(plan):
                if step is not None and step[0] == 2:
                    value = jnp.where(d == at, around, value)
            got.append(send(value, target))
        own_block = jnp.where(d == 0, same, beside)
        odd = got[0] + got[2]
        straight = odd + jnp.where(d == 2, 0, own_block + got[1])
        turned = jnp.where(d == 2, 0, odd) + got[1] + got[3]

    with jax.named_scope("place"):
        scale = 1.0 / (NXW * NZ)
        mine, theirs = straight[0] * scale, straight[1] * scale
        received = send(theirs, across)
        turned = turned * scale
        first, second = jnp.where(c == 0, turned[0], turned[1]), jnp.where(c == 0, turned[1], turned[0])
        result = []
        for part in (slice(0, own), slice(own, 2 * own)):
            across_cores = jnp.concatenate([first[:, part].T, second[:, part].T], axis=1)
            lower, upper = mine[:, part], received[:, part]
            along = jnp.concatenate([jnp.where(c == 0, lower, upper), jnp.where(c == 0, upper, lower)], axis=1)
            result.append(jnp.where(d == 3, across_cores, jnp.where(d == 2, along + across_cores, along)))
    return result[0], result[1]


def solution(mesh):
    placed = (P(None, None, "span", "snap"),)
    return jax.shard_map(
        body,
        mesh=mesh,
        in_specs=placed,
        out_specs=(P("snap", "span"), P("snap", "span")),
        check_vma=False,
    )
```

```python
import functools

import jax
import jax.numpy as jnp
from jax import lax
from jax.sharding import PartitionSpec as P

NZ = 1536
NXW = 12
AXES = ("snap", "span")
SWAPS = ((), (2, 3), (0,))
COORDS = [
    (x, h, c, y, l)
    for x in range(4) for h in range(2) for c in range(2) for y in range(4) for l in range(2)
]


def place(x, h, c, y, l):
    return (x % 4 * 4 + h * 2 + c) * 8 + y % 4 * 2 + l


def after(value, *others):
    return lax.optimization_barrier((value, *others))[0]


def send(value, target, behind=()):
    if behind:
        value = after(value, *behind)
    pairs = []
    for at in COORDS:
        to = target(*at)
        if to is not None:
            pairs.append((place(*at), place(*to)))
    return lax.ppermute(value, AXES, pairs)


def inner(left, right):
    return lax.dot_general(
        left, right, (((0,), (0,)), ((), ())), preferred_element_type=jnp.float32
    )


def up(x, h, c, y, l):
    return x + 1, h, c, y, l


def down(x, h, c, y, l):
    return x - 1, h, c, y, l


def across(x, h, c, y, l):
    return x, h, 1 - c, y, l


def body(snapshots):
    comps, rows, depth, own = snapshots.shape
    quarter = rows // 4
    count = comps * quarter * depth
    snap, span = lax.axis_index("snap"), lax.axis_index("span")
    x, h, c = snap // 4, snap // 2 % 2, snap % 2
    y, l = span // 2, span % 2
    m = y // 2

    def part(side, group):
        return lax.dynamic_slice_in_dim(snapshots, (side * 2 + group) * quarter, quarter, axis=1)

    sign = jnp.array([1.0, 1.0, -1.0], jnp.bfloat16).reshape(3, 1, 1, 1)
    swap = jnp.flip(jnp.eye(depth, dtype=jnp.bfloat16), 0)

    def reflect(piece):
        turned = lax.dot_general(piece, swap, (((2,), (1,)), ((), ())), preferred_element_type=jnp.bfloat16)
        return jnp.swapaxes(turned, 2, 3) * sign

    flat = lambda piece: piece.reshape(count, own)
    def above(x, h, c, y, l):
        return (x + 1, h, c, y, l) if (y - x - 1) % 4 < 2 else None

    with jax.named_scope("rows"):
        s1 = flat(send(part(m, 1 - h), lambda x, h, c, y, l: (x, 1 - h, c, y, l)))
        t0 = send(part(1 - m, h), lambda x, h, c, y, l: (x, h, c, 3 - y, 1 - l))
        t1 = send(part(1 - m, 1 - h), lambda x, h, c, y, l: (x, 1 - h, c, 3 - y, 1 - l))
        t0, t1 = flat(reflect(t0)), flat(reflect(t1))
        s0 = after(flat(part(m, h)), swap)
    with jax.named_scope("first"):
        n0 = send(s0, down)
        p0 = send(s0, above)
        n1 = send(t0, down, [n0])
        p1 = send(t0, above, [p0])
    with jax.named_scope("second"):
        pair = jnp.concatenate([s1, t1])
        n2 = send(pair, down)
        p2 = send(pair, above)
        c0, c1, c2 = send(s0, across, [s1, t1, n1, p1]), send(t0, across, [s1, t1, n1, p1]), send(pair, across)
        s0, t0, n1, p0, p1 = after((s0, t0, n1, p0, p1), c0, c1, c2)
        q0, q1 = send(p0, across), send(p1, across)
        p0, p1 = after((p0, p1), q0, q1)

    def columns(name, *cores):
        with jax.named_scope(name):
            result = jnp.zeros((2 * count, 4 * own), jnp.bfloat16)
            for i, (s, t, st) in enumerate(cores):
                result = lax.dynamic_update_slice(result, s, (0, 2 * i * own))
                result = lax.dynamic_update_slice(result, t, (count, 2 * i * own))
                result = lax.dynamic_update_slice(result, st[:count], (0, (2 * i + 1) * own))
                result = lax.dynamic_update_slice(result, st[count:], (count, (2 * i + 1) * own))
            return result

    left = columns("left", (s0, t0, pair), (c0, c1, c2))

    def products(lhs, s, t):
        right = jnp.concatenate(
            [jnp.concatenate([s, t], axis=1), jnp.concatenate([t, s], axis=1)], axis=0
        )
        return inner(lhs, right).reshape(2, 2, own, 2 * own)

    d = (y - x) % 4

    def over_z(first, second, behind, active=lambda *at: True, swaps=()):
        swap = functools.reduce(jnp.logical_or, [d == at for at in swaps], jnp.zeros((), bool))

        def block(k):
            to = (2 * h + l + k) % 4
            row, column = jnp.where(swap, to % 2, to // 2), jnp.where(swap, to // 2, to % 2)
            pick = lambda both: lax.dynamic_index_in_dim(both, row ^ h, 1, keepdims=False)
            return jnp.where(column ^ h == 0, pick(first), pick(second))

        total = block(0)
        for k in (1, 3, 2):
            def target(x, h, c, y, l, k=k):
                to = (2 * h + l + k) % 4
                return (x, to // 2, c, y, to % 2) if active(x, h, c, y, l) else None
            total = total + send(block(k), target, behind)
        return total

    with jax.named_scope("same"):
        same = over_z(products(left, s0, t0), products(left, pair[:count], pair[count:]), [])
    with jax.named_scope("beside"):
        n2 = after(n2, same)
        beside = over_z(products(left, n0, n1), products(left, n2[:count], n2[count:]), [], swaps=SWAPS[1])
    with jax.named_scope("around"):
        p2 = after(p2, same)
        q2 = send(p2, across)
        previous = columns("previous", (p0, p1, p2), (q0, q1, q2))
        around = over_z(
            products(previous, n0, n1),
            products(previous, n2[:count], n2[count:]),
            [],
            lambda x, h, c, y, l: (y - x) % 4 < 2,
            SWAPS[2],
        )

    same, beside = lax.optimization_barrier((same, beside))
    mixed = lax.optimization_barrier(tuple(jnp.where(d == at, same, beside) for at in (1, 3, 2)))

    rounds = (
        ((2, False), (0, False), (1, True), (1, False)),
        ((2, True), (1, True), None, None),
        ((1, True), (2, False), (1, False), (0, False)),
        ((1, False), (2, True), (0, False), (1, True)),
    )
    with jax.named_scope("over_y"):
        got = []
        for plan in rounds:
            def target(x, h, c, y, l, plan=plan):
                if plan[(y - x) % 4] is None:
                    return None
                block, turn = plan[(y - x) % 4]
                row, column = ((x, x), (x, x + 1), (x - 1, x + 1))[block]
                if turn:
                    row, column = column, row
                if turn != ((y - x) % 4 in SWAPS[block]):
                    h, l = l, h
                return row % 4, h, c, column, l
            value = (mixed[0], beside, mixed[1], mixed[2])[len(got)]
            for at, step in enumerate(plan):
                if step is not None and step[0] == 2:
                    value = jnp.where(d == at, around, value)
            got.append(send(value, target))
        own_block = jnp.where(d == 0, same, beside)
        got = got[2:] + got[:2]
        odd = got[0] + got[2]
        straight = odd + jnp.where(d == 2, 0, own_block + got[1])
        turned = jnp.where(d == 2, 0, odd) + got[1] + got[3]

    with jax.named_scope("place"):
        scale = 1.0 / (NXW * NZ)
        mine, theirs = straight[0] * scale, straight[1] * scale
        received = send(theirs, across)
        turned = turned * scale
        first, second = jnp.where(c == 0, turned[0], turned[1]), jnp.where(c == 0, turned[1], turned[0])
        result = []
        for part in (slice(0, own), slice(own, 2 * own)):
            across_cores = jnp.concatenate([first[:, part].T, second[:, part].T], axis=1)
            lower, upper = mine[:, part], received[:, part]
            along = jnp.concatenate([jnp.where(c == 0, lower, upper), jnp.where(c == 0, upper, lower)], axis=1)
            result.append(jnp.where(d == 3, across_cores, jnp.where(d == 2, along + across_cores, along)))
    return result[0], result[1]


def solution(mesh):
    placed = (P(None, None, "span", "snap"),)
    return jax.shard_map(
        body,
        mesh=mesh,
        in_specs=placed,
        out_specs=(P("snap", "span"), P("snap", "span")),
        check_vma=False,
    )
```

```python
import functools

import jax
import jax.numpy as jnp
from jax import lax
from jax.sharding import PartitionSpec as P

NZ = 1536
NXW = 12
AXES = ("snap", "span")
SWAPS = ((), (2, 3), (0,))
COORDS = [
    (x, h, c, y, l)
    for x in range(4) for h in range(2) for c in range(2) for y in range(4) for l in range(2)
]


def place(x, h, c, y, l):
    return (x % 4 * 4 + h * 2 + c) * 8 + y % 4 * 2 + l


def after(value, *others):
    return lax.optimization_barrier((value, *others))[0]


def send(value, target, behind=()):
    if behind:
        value = after(value, *behind)
    pairs = []
    for at in COORDS:
        to = target(*at)
        if to is not None:
            pairs.append((place(*at), place(*to)))
    return lax.ppermute(value, AXES, pairs)


def inner(left, right):
    return lax.dot_general(
        left, right, (((0,), (0,)), ((), ())), preferred_element_type=jnp.float32
    )


def up(x, h, c, y, l):
    return x + 1, h, c, y, l


def down(x, h, c, y, l):
    return x - 1, h, c, y, l


def across(x, h, c, y, l):
    return x, h, 1 - c, y, l


def body(snapshots):
    comps, rows, depth, own = snapshots.shape
    quarter = rows // 4
    count = comps * quarter * depth
    snap, span = lax.axis_index("snap"), lax.axis_index("span")
    x, h, c = snap // 4, snap // 2 % 2, snap % 2
    y, l = span // 2, span % 2
    m = y // 2

    def part(side, group):
        return lax.dynamic_slice_in_dim(snapshots, (side * 2 + group) * quarter, quarter, axis=1)

    sign = jnp.array([1.0, 1.0, -1.0], jnp.bfloat16).reshape(3, 1, 1, 1)
    swap = jnp.flip(jnp.eye(depth, dtype=jnp.bfloat16), 0)

    def reflect(piece):
        turned = lax.dot_general(piece, swap, (((2,), (1,)), ((), ())), preferred_element_type=jnp.bfloat16)
        return jnp.swapaxes(turned, 2, 3) * sign

    flat = lambda piece: piece.reshape(count, own)
    def above(x, h, c, y, l):
        return (x + 1, h, c, y, l) if (y - x - 1) % 4 < 2 else None

    with jax.named_scope("rows"):
        s1 = flat(send(part(m, 1 - h), lambda x, h, c, y, l: (x, 1 - h, c, y, l)))
        t0 = send(part(1 - m, h), lambda x, h, c, y, l: (x, h, c, 3 - y, 1 - l))
        t1 = send(part(1 - m, 1 - h), lambda x, h, c, y, l: (x, 1 - h, c, 3 - y, 1 - l))
        t0, t1 = flat(reflect(t0)), flat(reflect(t1))
        s0 = after(flat(part(m, h)), swap)
    with jax.named_scope("first"):
        n0 = send(s0, down)
        p0 = send(s0, above)
        n1 = send(t0, down, [n0])
        p1 = send(t0, above, [p0])
    with jax.named_scope("second"):
        pair = jnp.concatenate([s1, t1])
        n2 = send(pair, down)
        p2 = send(pair, above)
        c0, c1, c2 = send(s0, across, [s1, t1, n1, p1]), send(t0, across, [s1, t1, n1, p1]), send(pair, across)
        s0, t0, n1, p0, p1 = after((s0, t0, n1, p0, p1), c0, c1, c2)
        q0, q1 = send(p0, across), send(p1, across)
        p0, p1 = after((p0, p1), q0, q1)

    def columns(name, *cores):
        with jax.named_scope(name):
            result = jnp.zeros((2 * count, 4 * own), jnp.bfloat16)
            for i, (s, t, st) in enumerate(cores):
                result = lax.dynamic_update_slice(result, s, (0, 2 * i * own))
                result = lax.dynamic_update_slice(result, t, (count, 2 * i * own))
                result = lax.dynamic_update_slice(result, st[:count], (0, (2 * i + 1) * own))
                result = lax.dynamic_update_slice(result, st[count:], (count, (2 * i + 1) * own))
            return result

    left = columns("left", (s0, t0, pair), (c0, c1, c2))

    def products(lhs, s, t):
        right = jnp.concatenate(
            [jnp.concatenate([s, t], axis=1), jnp.concatenate([t, s], axis=1)], axis=0
        )
        return inner(lhs, right).reshape(2, 2, own, 2 * own)

    d = (y - x) % 4

    def over_z(first, second, behind, active=lambda *at: True, swaps=()):
        swap = functools.reduce(jnp.logical_or, [d == at for at in swaps], jnp.zeros((), bool))

        def block(k):
            to = (2 * h + l + k) % 4
            row, column = jnp.where(swap, to % 2, to // 2), jnp.where(swap, to // 2, to % 2)
            pick = lambda both: lax.dynamic_index_in_dim(both, row ^ h, 1, keepdims=False)
            return jnp.where(column ^ h == 0, pick(first), pick(second))

        total = block(0)
        for k in (1, 3, 2) if active(0, 0, 0, 2, 0) else (3, 1, 2):
            def target(x, h, c, y, l, k=k):
                to = (2 * h + l + k) % 4
                return (x, to // 2, c, y, to % 2) if active(x, h, c, y, l) else None
            total = total + send(block(k), target, behind)
        return total

    with jax.named_scope("same"):
        same = over_z(products(left, s0, t0), products(left, pair[:count], pair[count:]), [])
    with jax.named_scope("beside"):
        n2 = after(n2, same)
        beside = over_z(products(left, n0, n1), products(left, n2[:count], n2[count:]), [], swaps=SWAPS[1])
    with jax.named_scope("around"):
        p2 = after(p2, same)
        q2 = send(p2, across)
        previous = columns("previous", (p0, p1, p2), (q0, q1, q2))
        around = over_z(
            products(previous, n0, n1),
            products(previous, n2[:count], n2[count:]),
            [],
            lambda x, h, c, y, l: (y - x) % 4 < 2,
            SWAPS[2],
        )

    same, beside = lax.optimization_barrier((same, beside))
    mixed = lax.optimization_barrier(tuple(jnp.where(d == at, same, beside) for at in (1, 3, 2)))

    rounds = (
        ((2, False), (0, False), (1, True), (1, False)),
        ((2, True), (1, True), None, None),
        ((1, True), (2, False), (1, False), (0, False)),
        ((1, False), (2, True), (0, False), (1, True)),
    )
    with jax.named_scope("over_y"):
        got = []
        for plan in rounds:
            def target(x, h, c, y, l, plan=plan):
                if plan[(y - x) % 4] is None:
                    return None
                block, turn = plan[(y - x) % 4]
                row, column = ((x, x), (x, x + 1), (x - 1, x + 1))[block]
                if turn:
                    row, column = column, row
                if turn != ((y - x) % 4 in SWAPS[block]):
                    h, l = l, h
                return row % 4, h, c, column, l
            value = (mixed[0], beside, mixed[1], mixed[2])[len(got)]
            for at, step in enumerate(plan):
                if step is not None and step[0] == 2:
                    value = jnp.where(d == at, around, value)
            got.append(send(value, target))
        own_block = jnp.where(d == 0, same, beside)
        got = got[2:] + got[:2]
        odd = got[0] + got[2]
        straight = odd + jnp.where(d == 2, 0, own_block + got[1])
        turned = jnp.where(d == 2, 0, odd) + got[1] + got[3]

    with jax.named_scope("place"):
        scale = 1.0 / (NXW * NZ)
        mine, theirs = straight[0] * scale, straight[1] * scale
        received = send(theirs, across)
        turned = turned * scale
        first, second = jnp.where(c == 0, turned[0], turned[1]), jnp.where(c == 0, turned[1], turned[0])
        result = []
        for part in (slice(0, own), slice(own, 2 * own)):
            across_cores = jnp.concatenate([first[:, part].T, second[:, part].T], axis=1)
            lower, upper = mine[:, part], received[:, part]
            along = jnp.concatenate([jnp.where(c == 0, lower, upper), jnp.where(c == 0, upper, lower)], axis=1)
            result.append(jnp.where(d == 3, across_cores, jnp.where(d == 2, along + across_cores, along)))
    return result[0], result[1]


def solution(mesh):
    placed = (P(None, None, "span", "snap"),)
    return jax.shard_map(
        body,
        mesh=mesh,
        in_specs=placed,
        out_specs=(P("snap", "span"), P("snap", "span")),
        check_vma=False,
    )
```
